128 devices in a mesh: fsdp: 32 (over z_lo, y, x), dp: 4 (over z_hi, core).
Axes of the slice: x: 4, y: 4, z: 4 (z_hi: 2, z_lo: 2; z = z_hi * 2 + z_lo), core: 2. Of those that a mesh axis runs over, the one named last changes fastest.
Arguments:
- tokens: bfloat16 [32768, 16384], P(('fsdp', 'dp')), may hold values from -0.75 to 0.75
- key_grads: bfloat16 [32768, 512], P(('fsdp', 'dp')), may hold values from -1 to 1
- old_param: bfloat16 [32768, 512], P('fsdp'), may hold values from -1.5 to 1.5
- old_first: float32 [32768, 512], P('fsdp'), may hold values from -6 to 6
- old_second: float32 [32768, 512], P('fsdp'), may hold values from 0.25 to 4
- old_home: int32 [1024], replicated, may hold values from 0 to 2047, as said below
Outputs:
- keys: bfloat16 [32768, 512], P(('fsdp', 'dp'))
- input_grads: bfloat16 [32768, 16384], P(('fsdp', 'dp'))
- new_param: bfloat16 [16384, 512], P('fsdp')
- new_first: float32 [16384, 512], P('fsdp')
- new_second: float32 [16384, 512], P('fsdp')
The draws below stay inside these ranges and needn't reach their ends.
Inputs may be any that keep to these rules, and one draw needn't show every extreme that they name: Values are distinct. Each fsdp index holds at most 64 blocks in the old layout, and some index holds exactly 64; at most 2 blocks go from one old owner to one new owner (block b's new owner is b // (1024 // 32), its old owner old_home[b] // 64), and some pair carries exactly 2.
All inputs are finite; a program needn't handle non-finite values.
Results may differ from the reference program's by a relative error of at most 0.004.
Values may be sent and summed in bfloat16 or wider, within the bound.
No kernel may reach another device: no remote copies, remote signals or barrier semaphores. Data moves between devices by JAX's collectives and lax.ppermute only.
A program may use at most 192 MiB of HBM per device.

```python
import math
import jax
import jax.numpy as jnp
from jax import lax

D = 16384
BR = 16
TOK_DEV = 256
C = 512
TOKENS = 32768
NB = 1024
OLD_SLOTS = 64
N_FSDP = 32
N_DP = 4


def draw_old_home(key, part):
    key = jax.random.fold_in(key, 7)
    key_rank, key_pos, key_slot = jax.random.split(key, 3)
    count_dev = N_FSDP
    per_dest = NB // count_dev
    base = NB // (count_dev * count_dev)
    quarter = count_dev // 4
    lighter = count_dev - quarter
    rank_source = jax.random.permutation(key_rank, count_dev)
    ranks = jnp.arange(count_dev)[:, None]
    dests = jnp.arange(count_dev)[None, :]
    window = (ranks - quarter - dests * quarter) % lighter
    dropped = (ranks >= quarter) & (window < quarter)
    counts = jnp.where(ranks < quarter, 2 * base, jnp.where(dropped, 0, base)).astype(jnp.int32)
    col_start = jnp.cumsum(counts, axis=0) - counts
    row_start = jnp.cumsum(counts, axis=1) - counts
    positions = jax.vmap(lambda k: jax.random.permutation(k, per_dest))(jax.random.split(key_pos, count_dev))
    starts_by_dest = col_start.T
    rank_of = jnp.sum((starts_by_dest[:, None, :] <= positions[:, :, None]).astype(jnp.int32), axis=2) - 1
    dest_index = jnp.arange(count_dev)[:, None]
    within = positions - starts_by_dest[dest_index, rank_of]
    source = rank_source[rank_of]
    order_index = row_start[rank_of, dest_index] + within
    slot_perm = jax.vmap(lambda k: jax.random.permutation(k, OLD_SLOTS))(jax.random.split(key_slot, count_dev))
    slot = slot_perm[source, order_index]
    return (source * OLD_SLOTS + slot).reshape(NB).astype(jnp.int32)


def with_spikes(drawn, rng, source, target, shards_of, factor):
    owner, partner = [(jnp.arange(drawn.shape[position]) // (drawn.shape[position] // shards_of)).reshape([-1 if axis == position else 1 for axis in range(drawn.ndim)]) for position in (source, target)]
    chosen = jax.random.permutation(rng, shards_of)[partner]
    strong = (owner == chosen) | (owner == (partner + shards_of // 2) % shards_of)
    return jnp.where(strong, factor * drawn, drawn)


def shard_levels(own_key, extent, cuts, low, top_value):
    factor_of = 1.0
    for dim, parts in cuts:
        draws = jax.random.uniform(jax.random.fold_in(jax.random.fold_in(own_key, 6), dim), (parts,), jnp.float32, low / len(cuts), top_value / len(cuts))
        factor_of = factor_of * jnp.repeat(jnp.exp(draws), extent[dim] // parts).reshape((-1,) + (1,) * (len(extent) - 1 - dim))
    return factor_of


def noise(rng, extent, deviation, most, cuts=(), dtype=jnp.bfloat16):
    factor_of = shard_levels(rng, extent, cuts, -0.22, 0.18) if cuts else 1.0
    array = jax.random.normal(rng, extent, jnp.float32) * deviation * factor_of
    return jnp.minimum(jnp.maximum(array, -most), most).astype(dtype)


def noise_with(own_key, shape, width, reach, cuts, heavy, dtype=jnp.bfloat16):
    array = width * jax.random.normal(own_key, shape, jnp.float32)
    if cuts:
        array = array * shard_levels(own_key, shape, cuts, -0.22, 0.18)
    return jnp.clip(with_spikes(array, jax.random.fold_in(own_key, 3), *heavy), -reach, reach).astype(dtype)


def setup_inputs(seed: int = 0) -> dict:
    key_of = jax.random.split(jax.random.key(seed), 7)
    return {
        "tokens": noise_with(key_of[0], (TOKENS, D), (C ** 0.25 * (D * TOKENS) ** -0.25), 0.75, ((0, 128),), (0, 1, 128, 5.5)),
        "key_grads": noise(key_of[1], (TOKENS, C), ((C * TOKENS // D) ** 0.5) ** -0.5, 1.0, ((0, 128),)),
        "old_param": noise(key_of[2], (N_FSDP * OLD_SLOTS * BR, C), ((C * D // TOKENS) ** 0.5) ** -0.5, 1.5, ((0, 32),)),
        "old_first": noise(key_of[3], (N_FSDP * OLD_SLOTS * BR, C), 1.0, 6.0, ((0, 32),), jnp.float32),
        "old_second": jnp.clip(jnp.exp(math.log(4.0) - 2.7725887 * jax.random.uniform(key_of[4], (N_FSDP * OLD_SLOTS * BR, C), jnp.float32) ** shard_levels(key_of[4], (N_FSDP * OLD_SLOTS * BR, C), ((0, 32),), -0.2, 0.2)), 0.25, 4.0),
        "old_home": draw_old_home(jax.random.fold_in(key_of[6], 71), 0),
    }


beta_first = 0.9
beta_second = 0.95
eps_adam = 1e-08
learn_rate = 0.001
decay_rate = 0.1
bias_first = 1.0 - 0.9 ** 10
bias_second = 1.0 - 0.95 ** 10

def relayout(buffer, old_home):
    blocks = buffer.reshape(N_FSDP * OLD_SLOTS, BR, C)
    return jnp.take(blocks, old_home.astype(jnp.int32), axis=0).reshape(D, C)

def reference(tokens, key_grads, old_param, old_first, old_second, old_home):
    weight = relayout(old_param, old_home)
    first = relayout(old_first, old_home)
    second = relayout(old_second, old_home)
    keys = jnp.dot(tokens, weight, preferred_element_type=jnp.float32).astype(jnp.bfloat16)
    input_grads = jnp.dot(key_grads, weight.T, preferred_element_type=jnp.float32).astype(jnp.bfloat16)
    devices_all = N_FSDP * N_DP
    token_blocks = tokens.reshape(devices_all, TOK_DEV, D)
    grad_blocks = key_grads.reshape(devices_all, TOK_DEV, C)

    def add_term(total, pieces):
        part = jnp.dot(pieces[0].T, pieces[1], preferred_element_type=jnp.float32)
        part = lax.optimization_barrier(part.astype(jnp.bfloat16))
        return (total + part.astype(jnp.float32), None)
    gradient, _ = lax.scan(add_term, jnp.zeros((D, C), jnp.float32), (token_blocks, grad_blocks))
    new_first = beta_first * first + (1.0 - beta_first) * gradient
    new_second = beta_second * second + (1.0 - beta_second) * gradient * gradient
    weight_wide = weight.astype(jnp.float32)
    update = new_first / bias_first / (jnp.sqrt(new_second / bias_second) + eps_adam) + decay_rate * weight_wide
    new_param = (weight_wide - learn_rate * update).astype(jnp.bfloat16)
    return (keys, input_grads, new_param, new_first, new_second)
```

```python
import functools
import itertools

import jax
import jax.numpy as jnp
from jax import lax
from jax.experimental import pallas as pl
from jax.experimental.pallas import tpu as pltpu
from jax.sharding import PartitionSpec as P

BR = 16
C = 512
HALF = 256
QUARTER = 128
BIG = 352
SMALL = C - BIG
TOK = 256
D = 16384
NF = 32

beta_first = 0.9
beta_second = 0.95
eps_adam = 1e-08
learn_rate = 0.001
decay_rate = 0.1
bias_first = 1.0 - 0.9**10
bias_second = 1.0 - 0.95**10

AXES = ("fsdp", "dp")
bf16 = jnp.bfloat16
f32 = jnp.float32
ANY = pl.BlockSpec(memory_space=pl.ANY)
SMEM = pl.BlockSpec(memory_space=pltpu.SMEM)
VMEM = pl.BlockSpec(memory_space=pltpu.VMEM)


def device_number(x, y, zl, zh, core):
    return (((zl * 4 + y) * 4 + x) * 2 + zh) * 2 + core


def shift_pairs(axis_of_core, shift):
    pairs = []
    for x, y, zl, zh, core in itertools.product(range(4), range(4), range(2), range(2), range(2)):
        to = {"x": x, "y": y, "l": zl, "h": zh, "c": core}
        axis = axis_of_core[core]
        to[axis] = (to[axis] + shift) % (4 if axis in "xy" else 2)
        pairs.append(
            (
                device_number(x, y, zl, zh, core),
                device_number(to["x"], to["y"], to["l"], to["h"], to["c"]),
            )
        )
    return pairs


def send(array, axis_of_core, shift=1):
    return lax.ppermute(array, AXES, shift_pairs(axis_of_core, shift))


OUTER = "xy"
INNER = "yx"
PAIR = "ll"
REPLICA = "hh"
CORE = "cc"


def split_kernel(place, tokens, key_grads, out, sem):
    core = place[3]
    copies = []
    for i in range(NF):
        at = pl.multiple_of(i * C + (1 - core) * HALF, HALF)
        copies.append(
            pltpu.make_async_copy(
                tokens.at[:, pl.ds(at, HALF)], out.at[:, pl.ds(i * HALF, HALF)], sem.at[i]
            )
        )
    copies.append(pltpu.make_async_copy(key_grads, out.at[:, pl.ds(D // 2, C)], sem.at[NF]))
    for copy in copies:
        copy.start()
    for copy in copies:
        copy.wait()


def split_tokens(place, tokens, key_grads):
    return pl.pallas_call(
        split_kernel,
        out_shape=jax.ShapeDtypeStruct((TOK, D // 2 + C), bf16),
        in_specs=[SMEM, ANY, ANY],
        out_specs=ANY,
        scratch_shapes=[pltpu.SemaphoreType.DMA((NF + 1,))],
        cost_estimate=pl.CostEstimate(flops=0, bytes_accessed=2**23, transcendentals=0),
    )(place, tokens, key_grads)


def pack_kernel(place, table, param, first, second, out):
    def body(k, carry):
        src = pl.multiple_of(table[k] * BR, BR)
        dst = pl.multiple_of(k * BR, BR)
        out[pl.ds(dst, BR), :HALF] = param[pl.ds(src, BR), :]
        out[pl.ds(dst, BR), HALF : HALF + QUARTER] = first[pl.ds(src, BR), :].astype(bf16)
        out[pl.ds(dst, BR), HALF + QUARTER :] = second[pl.ds(src, BR), :].astype(bf16)
        return carry

    lax.fori_loop(0, 2 * NF, body, 0, unroll=4)


def pack(place, table, param, first, second):
    rows = param.shape[0]
    quarter = lambda i, place, table: (0, place[3] * 2 + place[4])
    return pl.pallas_call(
        pack_kernel,
        out_shape=jax.ShapeDtypeStruct((2 * NF * BR, C), bf16),
        grid_spec=pltpu.PrefetchScalarGridSpec(
            num_scalar_prefetch=2,
            grid=(1,),
            in_specs=[
                pl.BlockSpec((rows, HALF), lambda i, place, table: (0, place[3])),
                pl.BlockSpec((rows, QUARTER), quarter),
                pl.BlockSpec((rows, QUARTER), quarter),
            ],
            out_specs=pl.BlockSpec((2 * NF * BR, C), lambda i, place, table: (0, 0)),
        ),
        compiler_params=pltpu.CompilerParams(vmem_limit_bytes=2**24),
        cost_estimate=pl.CostEstimate(flops=0, bytes_accessed=3 * 2**20, transcendentals=0),
    )(place, table, param, first, second)


def unpack_kernel(rows_taken, got, weight, moments):
    def body(k, carry):
        src = pl.multiple_of(rows_taken[k] * BR, BR)
        dst = pl.multiple_of(k * BR, BR)
        weight[pl.ds(dst, BR), :] = got[pl.ds(src, BR), :HALF]
        moments[pl.ds(dst, BR), :] = got[pl.ds(src, BR), HALF:]
        return carry

    lax.fori_loop(0, NF, body, 0, unroll=4)


def unpack(rows_taken, got):
    half = jax.ShapeDtypeStruct((C, HALF), bf16)
    return pl.pallas_call(
        unpack_kernel,
        out_shape=(half, half),
        in_specs=[SMEM, VMEM],
        out_specs=(VMEM, VMEM),
        compiler_params=pltpu.CompilerParams(vmem_limit_bytes=2**23),
        cost_estimate=pl.CostEstimate(flops=0, bytes_accessed=2 * 2**20, transcendentals=0),
    )(rows_taken, got)


def target_index(place, core, outer, pair, inner, sign):
    x, y, zl = place[0], place[1], place[2]
    along_x = jnp.where(core == 0, outer, inner)
    along_y = jnp.where(core == 0, inner, outer)
    to_x = lax.rem(x + sign * along_x + 4, 4)
    to_y = lax.rem(y + sign * along_y + 4, 4)
    to_z = lax.rem(zl + pair, 2)
    return (to_z * 4 + to_y) * 4 + to_x


def gradient_kernel(place, tokens, theirs, key_grads, *refs):
    big, small = refs[0:4], refs[4:6]
    held, made, other_grads, grads_t, sem_in, sem_grads, sem_big, sem_small = refs[6:]
    core = place[3]
    grads_copy = pltpu.make_async_copy(
        theirs.at[:, pl.ds(D // 2, C)], other_grads, sem_grads
    )
    grads_copy.start()

    def loads(i, f):
        mine = pltpu.make_async_copy(
            tokens.at[:, pl.ds(pl.multiple_of(f * C + core * HALF, HALF), HALF)],
            held.at[i, pl.ds(0, TOK)],
            sem_in.at[0, i],
        )
        other = pltpu.make_async_copy(
            theirs.at[:, pl.ds(pl.multiple_of(f * HALF, HALF), HALF)],
            held.at[i, pl.ds(TOK, TOK)],
            sem_in.at[1, i],
        )
        return mine, other

    def start(i, carry):
        outer, rest = lax.div(i, 8), lax.rem(i, 8)
        f = target_index(place, core, outer, lax.div(rest, 4), lax.rem(rest, 4), 1)
        for copy in loads(i, f):
            copy.start()
        return carry

    lax.fori_loop(0, NF, start, 0)
    grads_t[:, :TOK] = key_grads[...].T
    grads_copy.wait()
    grads_t[:, TOK:] = other_grads[...].T
    for outer in range(4):
        for pair in range(2):

            def body(inner, carry, outer=outer, pair=pair):
                i = outer * 8 + pair * 4 + inner
                for copy in loads(i, 0):
                    copy.wait()
                made[i] = jnp.dot(
                    grads_t[...], held[i], preferred_element_type=f32
                ).astype(bf16)
                pltpu.make_async_copy(
                    made.at[i, pl.ds(0, BIG)], big[outer].at[pair, inner], sem_big.at[outer]
                ).start()
                pltpu.make_async_copy(
                    made.at[i, pl.ds(BIG, SMALL)], small[pair].at[outer, inner], sem_small.at[pair]
                ).start()
                return carry

            lax.fori_loop(0, 4, body, 0)
    for outer in range(4):
        pltpu.make_async_copy(big[outer], big[outer], sem_big.at[outer]).wait()
    for pair in range(2):
        pltpu.make_async_copy(small[pair], small[pair], sem_small.at[pair]).wait()


def gradient_terms(place, tokens, theirs, key_grads):
    big = jax.ShapeDtypeStruct((2, 4, BIG, HALF), bf16)
    small = jax.ShapeDtypeStruct((4, 4, SMALL, HALF), bf16)
    return pl.pallas_call(
        gradient_kernel,
        out_shape=(big,) * 4 + (small,) * 2,
        in_specs=[SMEM, ANY, ANY, VMEM],
        out_specs=(ANY,) * 6,
        scratch_shapes=[
            pltpu.VMEM((NF, 2 * TOK, HALF), bf16),
            pltpu.VMEM((NF, C, HALF), bf16),
            pltpu.VMEM((TOK, C), bf16),
            pltpu.VMEM((C, 2 * TOK), bf16),
            pltpu.SemaphoreType.DMA((2, NF)),
            pltpu.SemaphoreType.DMA,
            pltpu.SemaphoreType.DMA((4,)),
            pltpu.SemaphoreType.DMA((2,)),
        ],
        compiler_params=pltpu.CompilerParams(vmem_limit_bytes=28 * 2**20),
        cost_estimate=pl.CostEstimate(
            flops=2 * 512 * 512 * 8192, bytes_accessed=2**24, transcendentals=0
        ),
    )(place, tokens, theirs, key_grads)


def final_kernel(place, tokens, key_grads, *refs):
    big, small = (refs[0:4], refs[6:10]), (refs[4:6], refs[10:12])
    keys, input_grads = refs[12:14]
    weight, held, made, total, sem_w, sem_in, sem_out = refs[14:]
    core = place[3]

    def at(i):
        sx, rest = lax.div(i, 8), lax.rem(i, 8)
        t, sy = lax.div(rest, 4), lax.rem(rest, 4)
        return sx, t, sy, target_index(place, 0, sx, t, sy, -1)

    def pieces(i, of, outer_big, outer_small, own_core, outer, t, inner):
        col = pl.ds(pl.multiple_of(own_core * HALF, HALF), HALF)
        return (
            lambda: pltpu.make_async_copy(
                big[of][outer_big].at[t, inner],
                weight.at[i, pl.ds(0, BIG), col],
                sem_w.at[2 * of, i],
            ),
            lambda: pltpu.make_async_copy(
                small[of][outer_small].at[outer, inner],
                weight.at[i, pl.ds(BIG, SMALL), col],
                sem_w.at[2 * of + 1, i],
            ),
        )

    def start(i, carry):
        sx, t, sy, f = at(i)
        pltpu.make_async_copy(
            tokens.at[:, pl.ds(pl.multiple_of(f * C, C), C)], held.at[i], sem_in.at[i]
        ).start()
        for of in range(2):
            own_core = core if of == 0 else 1 - core
            outer = jnp.where(own_core == 0, sx, sy)
            inner = jnp.where(own_core == 0, sy, sx)
            for k in range(4):

                @pl.when(outer == k)
                def _(k=k, of=of, own_core=own_core, outer=outer, inner=inner):
                    pieces(i, of, k, 0, own_core, outer, t, inner)[0]().start()

            for k in range(2):

                @pl.when(t == k)
                def _(k=k, of=of, own_core=own_core, outer=outer, inner=inner):
                    pieces(i, of, 0, k, own_core, outer, t, inner)[1]().start()

        return carry

    lax.fori_loop(0, NF, start, 0)
    total[...] = jnp.zeros_like(total)

    def body(i, carry):
        _, _, _, f = at(i)
        pltpu.make_async_copy(tokens.at[:, pl.ds(0, C)], held.at[i], sem_in.at[i]).wait()
        for of in range(2):
            for copy in pieces(i, of, 0, 0, of, 0, 0, 0):
                copy().wait()
        total[...] += jnp.dot(held[i], weight[i], preferred_element_type=f32)
        made[i] = lax.dot_general(
            key_grads[...], weight[i], (((1,), (1,)), ((), ())), preferred_element_type=f32
        ).astype(bf16)
        pltpu.make_async_copy(
            made.at[i], input_grads.at[:, pl.ds(pl.multiple_of(f * C, C), C)], sem_out
        ).start()
        return carry

    lax.fori_loop(0, NF, body, 0)
    keys[...] = total[...].astype(bf16)
    pltpu.make_async_copy(input_grads, input_grads, sem_out).wait()


def final_products(place, tokens, key_grads, pieces):
    return pl.pallas_call(
        final_kernel,
        out_shape=(
            jax.ShapeDtypeStruct((TOK, C), bf16),
            jax.ShapeDtypeStruct((TOK, D), bf16),
        ),
        in_specs=[SMEM, ANY, VMEM] + [ANY] * 12,
        out_specs=(VMEM, ANY),
        scratch_shapes=[
            pltpu.VMEM((NF, C, C), bf16),
            pltpu.VMEM((NF, TOK, C), bf16),
            pltpu.VMEM((NF, TOK, C), bf16),
            pltpu.VMEM((TOK, C), f32),
            pltpu.SemaphoreType.DMA((4, NF)),
            pltpu.SemaphoreType.DMA((NF,)),
            pltpu.SemaphoreType.DMA,
        ],
        compiler_params=pltpu.CompilerParams(vmem_limit_bytes=44 * 2**20),
        cost_estimate=pl.CostEstimate(
            flops=4 * 256 * 512 * 16384, bytes_accessed=2**25, transcendentals=0
        ),
    )(place, tokens, key_grads, *pieces)


def routes(old_home, f, slots):
    home = old_home.reshape(NF, NF)
    source = home // slots
    idx = jnp.arange(NF)
    earlier = idx[None, :, None] > idx[None, None, :]
    same = source[:, :, None] == source[:, None, :]
    rank = jnp.sum((same & earlier).astype(jnp.int32), axis=2)
    mine = source == f
    slot = jnp.where(mine, home % slots, 0)
    table = jnp.stack([jnp.sum(jnp.where(rank == r, slot, 0), axis=1) for r in range(2)], axis=1)
    arrives = source * 2 + rank
    rows_taken = jnp.sum(jnp.where(idx[:, None] == f, arrives, 0), axis=0)
    return table.reshape(2 * NF), rows_taken


def add(*terms):
    total = terms[0].astype(f32)
    for term in terms[1:]:
        total = total + term.astype(f32)
    return total


def reduce_scatter(big, small):
    got_big = [send(big[s], OUTER, s) for s in (2, 1, 3)]
    got_small = send(small[1], PAIR)
    away = add(big[0][1], *[g[1] for g in got_big]).astype(bf16)
    got_away = send(away, PAIR)
    v = [add(small[0][s], got_small[s]).astype(bf16) for s in range(4)]
    got_v = [send(v[s], OUTER, s) for s in (2, 1, 3)]
    u = [
        add(big[0][0, s], *[g[0, s] for g in got_big], got_away[s]).astype(bf16) for s in range(4)
    ]
    w = [add(v[0][s], *[g[s] for g in got_v]).astype(bf16) for s in range(4)]
    whole = [jnp.concatenate([u[s], w[s]], axis=0) for s in range(4)]
    got = [send(whole[s], INNER, s) for s in (2, 1, 3)]
    return add(whole[0], *got)


def all_gather(seed):
    first = [seed] + [send(seed, INNER, s) for s in (1, 2, 3)]
    big = jnp.stack([p[:BIG] for p in first])
    small = jnp.stack([p[BIG:] for p in first])
    big = jnp.stack([big, send(big, PAIR)])
    small = jnp.stack([small] + [send(small, OUTER, s) for s in (1, 2, 3)])
    bigs = {s: send(big, OUTER, s) for s in (2, 1, 3)}
    return (big, bigs[1], bigs[2], bigs[3], small, send(small, PAIR))


def adamw_kernel(place, grads, weights, moments, *refs):
    grads_other, weights_other, moments_other, new_param, new_first, new_second = refs

    def update(core):
        for r in range(2):
            rows = pl.ds(r * HALF, HALF)
            turned = (grads if r == core else grads_other)[...].T
            for c in range(2):
                cols = pl.ds(c * HALF, HALF)
                m = moments if c == core else moments_other
                weight = (weights if c == core else weights_other)[rows, :].astype(f32)
                gradient = turned[:, c * HALF : (c + 1) * HALF]
                first = beta_first * m[rows, :HALF].astype(f32) + (1.0 - beta_first) * gradient
                second = (
                    beta_second * m[rows, HALF:].astype(f32)
                    + (1.0 - beta_second) * gradient * gradient
                )
                step = (
                    first / bias_first / (jnp.sqrt(second / bias_second) + eps_adam)
                    + decay_rate * weight
                )
                new_first[rows, cols] = first
                new_second[rows, cols] = second
                new_param[rows, cols] = (weight - learn_rate * step).astype(bf16)

    for core in range(2):
        pl.when(place[3] == core)(functools.partial(update, core))


def adamw(place, own, other):
    wide = jax.ShapeDtypeStruct((C, C), f32)
    return pl.pallas_call(
        adamw_kernel,
        out_shape=(jax.ShapeDtypeStruct((C, C), bf16), wide, wide),
        in_specs=[SMEM] + [VMEM] * 6,
        out_specs=(VMEM,) * 3,
        compiler_params=pltpu.CompilerParams(vmem_limit_bytes=2**24),
        cost_estimate=pl.CostEstimate(flops=2**22, bytes_accessed=6 * 2**20, transcendentals=2**18),
    )(place, *own, *other)


def ordered(index, own, other, axis):
    low = jnp.where(index == 0, own, other)
    high = jnp.where(index == 0, other, own)
    return jnp.concatenate([low, high], axis=axis)


def on_device(tokens, key_grads, old_param, old_first, old_second, old_home):
    f = lax.axis_index("fsdp").astype(jnp.int32)
    d = lax.axis_index("dp").astype(jnp.int32)
    core, zh = d % 2, d // 2
    place = jnp.stack([f % 4, (f // 4) % 4, f // 16, core, zh])

    theirs = send(split_tokens(place, tokens, key_grads), CORE)
    terms = gradient_terms(place, tokens, theirs, key_grads)

    table, rows_taken = routes(old_home, f, old_param.shape[0] // BR)
    packed = pack(place, table, old_param, old_first, old_second)
    got = lax.all_to_all(packed, "fsdp", split_axis=0, concat_axis=0, tiled=True)
    seed, moments = unpack(rows_taken, got)

    partial = reduce_scatter(terms[:4], terms[4:]).astype(bf16)
    own = all_gather(seed)
    other = tuple(send(p, CORE) for p in own)
    keys, input_grads = final_products(place, tokens, key_grads, own + other)

    moments_zh = send(moments, REPLICA)
    halves = jnp.concatenate(
        [
            ordered(zh, moments[:, :QUARTER], moments_zh[:, :QUARTER], 1),
            ordered(zh, moments[:, QUARTER:], moments_zh[:, QUARTER:], 1),
        ],
        axis=1,
    )
    halves_other = send(halves, CORE)
    seed_other = jnp.concatenate([other[0][0, 0], other[4][0, 0]], axis=0)

    gradient = partial.astype(f32) + send(partial, REPLICA).astype(f32)
    new_param, new_first, new_second = adamw(
        place, (gradient, seed, halves), (send(gradient, CORE), seed_other, halves_other)
    )
    return (keys, input_grads, new_param, new_first, new_second)


def solution(mesh):
    over_all = P(("fsdp", "dp"), None)
    over_fsdp = P("fsdp", None)
    return jax.shard_map(
        on_device,
        mesh=mesh,
        in_specs=(over_all, over_all, over_fsdp, over_fsdp, over_fsdp, P()),
        out_specs=(over_all, over_all, over_fsdp, over_fsdp, over_fsdp),
        check_vma=False,
    )
```

```python
import functools
import itertools

import jax
import jax.numpy as jnp
from jax import lax
from jax.experimental import pallas as pl
from jax.experimental.pallas import tpu as pltpu
from jax.sharding import PartitionSpec as P

BR = 16
C = 512
HALF = 256
QUARTER = 128
TOK = 256
D = 16384
NF = 32

beta_first = 0.9
beta_second = 0.95
eps_adam = 1e-08
learn_rate = 0.001
decay_rate = 0.1
bias_first = 1.0 - 0.9**10
bias_second = 1.0 - 0.95**10

AXES = ("fsdp", "dp")
bf16 = jnp.bfloat16
f32 = jnp.float32
ANY = pl.BlockSpec(memory_space=pl.ANY)
SMEM = pl.BlockSpec(memory_space=pltpu.SMEM)
VMEM = pl.BlockSpec(memory_space=pltpu.VMEM)
LIGHT = pl.CostEstimate(flops=0, bytes_accessed=1024, transcendentals=0)


def device_number(x, y, zl, zh, core):
    return (((zl * 4 + y) * 4 + x) * 2 + zh) * 2 + core


def shift_pairs(axis_of_core, shift):
    pairs = []
    for x, y, zl, zh, core in itertools.product(range(4), range(4), range(2), range(2), range(2)):
        to = {"x": x, "y": y, "l": zl, "h": zh, "c": core}
        axis = axis_of_core[core]
        to[axis] = (to[axis] + shift) % (4 if axis in "xy" else 2)
        pairs.append(
            (
                device_number(x, y, zl, zh, core),
                device_number(to["x"], to["y"], to["l"], to["h"], to["c"]),
            )
        )
    return pairs


def send(array, axis_of_core, shift=1):
    return lax.ppermute(array, AXES, shift_pairs(axis_of_core, shift))


OUTER = "xy"
INNER = "yx"
PAIR = "ll"
REPLICA = "hh"
CORE = "cc"


def split_kernel(place, tokens, key_grads, mine, out):
    core = place[3]
    for i in range(NF):
        at = lambda k: pl.ds(pl.multiple_of(i * C + k * HALF, HALF), HALF)
        mine[:, i * HALF : (i + 1) * HALF] = tokens[:, at(core)]
        out[:, i * HALF : (i + 1) * HALF] = tokens[:, at(1 - core)]
    out[:, D // 2 :] = key_grads[...]


def split_tokens(place, tokens, key_grads):
    rows = 32
    band = lambda width: pl.BlockSpec((rows, width), lambda i, place: (i, 0))
    return pl.pallas_call(
        split_kernel,
        out_shape=(
            jax.ShapeDtypeStruct((TOK, D // 2), bf16),
            jax.ShapeDtypeStruct((TOK, D // 2 + C), bf16),
        ),
        grid_spec=pltpu.PrefetchScalarGridSpec(
            num_scalar_prefetch=1,
            grid=(TOK // rows,),
            in_specs=[band(D), band(C)],
            out_specs=(band(D // 2), band(D // 2 + C)),
        ),
        compiler_params=pltpu.CompilerParams(vmem_limit_bytes=54 * 2**20),
        cost_estimate=LIGHT,
    )(place, tokens, key_grads)


def pack_kernel(place, table, param, first, second, out):
    def body(k, carry):
        src = pl.multiple_of(table[k] * BR, BR)
        dst = pl.multiple_of(k * BR, BR)
        out[pl.ds(dst, BR), :HALF] = param[pl.ds(src, BR), :]
        out[pl.ds(dst, BR), HALF : HALF + QUARTER] = first[pl.ds(src, BR), :].astype(bf16)
        out[pl.ds(dst, BR), HALF + QUARTER :] = second[pl.ds(src, BR), :].astype(bf16)
        return carry

    lax.fori_loop(0, 2 * NF, body, 0, unroll=4)


def pack(place, table, param, first, second):
    rows = param.shape[0]
    quarter = lambda i, place, table: (0, place[3] * 2 + place[4])
    return pl.pallas_call(
        pack_kernel,
        out_shape=jax.ShapeDtypeStruct((2 * NF * BR, C), bf16),
        grid_spec=pltpu.PrefetchScalarGridSpec(
            num_scalar_prefetch=2,
            grid=(1,),
            in_specs=[
                pl.BlockSpec((rows, HALF), lambda i, place, table: (0, place[3])),
                pl.BlockSpec((rows, QUARTER), quarter),
                pl.BlockSpec((rows, QUARTER), quarter),
            ],
            out_specs=pl.BlockSpec((2 * NF * BR, C), lambda i, place, table: (0, 0)),
        ),
        compiler_params=pltpu.CompilerParams(vmem_limit_bytes=2**24),
        cost_estimate=LIGHT,
    )(place, table, param, first, second)


def unpack_kernel(rows_taken, got, weight, moments):
    def body(k, carry):
        src = pl.multiple_of(rows_taken[k] * BR, BR)
        dst = pl.multiple_of(k * BR, BR)
        weight[pl.ds(dst, BR), :] = got[pl.ds(src, BR), :HALF]
        moments[pl.ds(dst, BR), :] = got[pl.ds(src, BR), HALF:]
        return carry

    lax.fori_loop(0, NF, body, 0, unroll=4)


def unpack(rows_taken, got):
    half = jax.ShapeDtypeStruct((C, HALF), bf16)
    return pl.pallas_call(
        unpack_kernel,
        out_shape=(half, half),
        in_specs=[SMEM, VMEM],
        out_specs=(VMEM, VMEM),
        compiler_params=pltpu.CompilerParams(vmem_limit_bytes=2**23),
        cost_estimate=LIGHT,
    )(rows_taken, got)


def target_index(place, core, outer, pair, inner, sign):
    x, y, zl = place[0], place[1], place[2]
    along_x = jnp.where(core == 0, outer, inner)
    along_y = jnp.where(core == 0, inner, outer)
    to_x = lax.rem(x + sign * along_x + 4, 4)
    to_y = lax.rem(y + sign * along_y + 4, 4)
    to_z = lax.rem(zl + pair, 2)
    return (to_z * 4 + to_y) * 4 + to_x


def gradient_term(place, mine, theirs, grads_t, outer, inner, pair):
    core = place[3]
    f = target_index(place, core, outer, pair, inner, 1)
    at = pl.ds(pl.multiple_of(f * HALF, HALF), HALF)
    return jnp.dot(
        grads_t[...],
        jnp.concatenate([mine[:, at], theirs[:, at]], axis=0),
        preferred_element_type=f32,
    ).astype(bf16)


def far_gradient_kernel(place, mine, theirs, key_grads, plus, minus, grads_t):
    grads_t[:, :TOK] = key_grads[...].T
    grads_t[:, TOK:] = theirs[:, D // 2 :].T
    for inner in range(2):
        for pair in range(2):
            term = functools.partial(gradient_term, place, mine, theirs, grads_t, 2)
            plus[inner, pair] = term(inner, pair)
            minus[inner, pair] = term(inner + 2, pair)


def near_gradient_kernel(place, mine, theirs, grads_t, *refs):
    for ref, (outer, first) in zip(refs, ((1, 2), (3, 0), (1, 0), (3, 2), (0, 0), (0, 2))):

        def body(inner, carry, ref=ref, outer=outer, first=first):
            for pair in range(2):
                ref[inner, pair] = gradient_term(
                    place, mine, theirs, grads_t, outer, first + inner, pair
                )
            return carry

        lax.fori_loop(0, 2, body, 0, unroll=2)


def gradient_terms(place, mine, theirs, key_grads):
    half = jax.ShapeDtypeStruct((2, 2, C, HALF), bf16)
    far_plus, far_minus, grads_t = pl.pallas_call(
        far_gradient_kernel,
        out_shape=(half, half, jax.ShapeDtypeStruct((C, 2 * TOK), bf16)),
        in_specs=[SMEM, VMEM, VMEM, VMEM],
        out_specs=(VMEM,) * 3,
        compiler_params=pltpu.CompilerParams(vmem_limit_bytes=20 * 2**20),
        cost_estimate=LIGHT,
    )(place, mine, theirs, key_grads)
    near = pl.pallas_call(
        near_gradient_kernel,
        out_shape=(half,) * 6,
        in_specs=[SMEM, VMEM, VMEM, VMEM],
        out_specs=(VMEM,) * 6,
        compiler_params=pltpu.CompilerParams(vmem_limit_bytes=24 * 2**20),
        cost_estimate=LIGHT,
    )(place, mine, theirs, grads_t)
    return (far_plus, far_minus) + tuple(near)


def is_near(outer, inner):
    return outer != 2 and inner != 2


def products(place, tokens, key_grads, piece, near, total, scratch, input_grads, start):
    held, weights, made, sem_in, sem_w, sem = scratch
    core = place[3]
    turn = lambda k: pl.ds(pl.multiple_of(k * HALF, HALF), HALF)
    steps = [
        (outer, inner, pair)
        for outer in range(4)
        for inner in range(4)
        for pair in range(2)
        if is_near(outer, inner) == near
    ]
    spots, loads = [], []
    for k, (outer, inner, pair) in enumerate(steps):
        f = target_index(place, core, outer, pair, inner, -1)
        spots.append(pl.ds(pl.multiple_of(f * C, C), C))
        sources = (piece(0, outer, inner, pair), piece(1, inner, outer, pair))
        loads.append(
            [
                pltpu.make_async_copy(sources[of], weights.at[k, of], sem_w.at[of, k])
                for of in range(2)
            ]
            + [pltpu.make_async_copy(tokens.at[:, spots[k]], held.at[k], sem_in.at[k])]
        )
        for copy in loads[k]:
            copy.start()
    grads = jnp.concatenate([key_grads[:, turn(core)], key_grads[:, turn(1 - core)]], axis=1)
    for k in range(len(steps)):
        for copy in loads[k]:
            copy.wait()
        weight = jnp.concatenate([weights[k, 0], weights[k, 1]], axis=1)
        made[k] = lax.dot_general(
            grads, weight, (((1,), (1,)), ((), ())), preferred_element_type=f32
        ).astype(bf16)
        pltpu.make_async_copy(made.at[k], input_grads.at[:, spots[k]], sem).start()
        term = jnp.dot(held[k], weight, preferred_element_type=f32)
        if k == 0:
            total[...] = term if start is None else start[...] + term
        else:
            total[...] += term
    pltpu.make_async_copy(made, made, sem).wait()


def piece_of(arrays, per_core):
    which = {0: 0, 1: 1, 3: 2}

    def piece(of, outer, inner, pair):
        if outer == 2:
            return arrays[per_core * of + 3 + inner // 2].at[inner % 2, pair]
        return arrays[per_core * of + which[outer]].at[inner, pair]

    return piece


def near_kernel(place, tokens, key_grads, *refs):
    arrays, (total, input_grads, *scratch) = refs[:6], refs[6:]
    piece = piece_of(arrays, 3)
    products(place, tokens, key_grads, piece, True, total, scratch, input_grads, None)


def far_kernel(place, tokens, key_grads, start, near_grads, *refs):
    arrays, (keys, input_grads, total, *scratch) = refs[:10], refs[10:]
    piece = piece_of(arrays, 5)
    products(place, tokens, key_grads, piece, False, total, scratch, input_grads, start)
    core = place[3]
    for of in range(2):
        owner = core if of == 0 else 1 - core
        keys[:, pl.ds(pl.multiple_of(owner * HALF, HALF), HALF)] = total[
            :, of * HALF : (of + 1) * HALF
        ].astype(bf16)


def product_scratch(steps):
    return [
        pltpu.VMEM((steps, TOK, C), bf16),
        pltpu.VMEM((steps, 2, C, HALF), bf16),
        pltpu.VMEM((steps, TOK, C), bf16),
        pltpu.SemaphoreType.DMA((steps,)),
        pltpu.SemaphoreType.DMA((2, steps)),
        pltpu.SemaphoreType.DMA,
    ]


def near_products(place, tokens, key_grads, pieces):
    return pl.pallas_call(
        near_kernel,
        out_shape=(
            jax.ShapeDtypeStruct((TOK, C), f32),
            jax.ShapeDtypeStruct((TOK, D), bf16),
        ),
        in_specs=[SMEM, ANY, VMEM] + [ANY] * 6,
        out_specs=(VMEM, ANY),
        scratch_shapes=product_scratch(18),
        compiler_params=pltpu.CompilerParams(vmem_limit_bytes=56 * 2**20),
        cost_estimate=LIGHT,
    )(place, tokens, key_grads, *pieces)


def far_products(place, tokens, key_grads, start, near_grads, pieces):
    return pl.pallas_call(
        far_kernel,
        out_shape=(
            jax.ShapeDtypeStruct((TOK, C), bf16),
            jax.ShapeDtypeStruct((TOK, D), bf16),
        ),
        in_specs=[SMEM, ANY, VMEM, VMEM] + [ANY] * 11,
        out_specs=(VMEM, ANY),
        scratch_shapes=[pltpu.VMEM((TOK, C), f32)] + product_scratch(14),
        input_output_aliases={4: 1},
        compiler_params=pltpu.CompilerParams(vmem_limit_bytes=56 * 2**20),
        cost_estimate=LIGHT,
    )(place, tokens, key_grads, start, near_grads, *pieces)


def routes(old_home, f, slots):
    home = old_home.reshape(NF, NF)
    source = home // slots
    idx = jnp.arange(NF)
    earlier = idx[None, :, None] > idx[None, None, :]
    same = source[:, :, None] == source[:, None, :]
    rank = jnp.sum((same & earlier).astype(jnp.int32), axis=2)
    mine = source == f
    slot = jnp.where(mine, home % slots, 0)
    table = jnp.stack([jnp.sum(jnp.where(rank == r, slot, 0), axis=1) for r in range(2)], axis=1)
    arrives = source * 2 + rank
    rows_taken = jnp.sum(jnp.where(idx[:, None] == f, arrives, 0), axis=0)
    return table.reshape(2 * NF), rows_taken


def add(*terms):
    total = terms[0].astype(f32)
    for term in terms[1:]:
        total = total + term.astype(f32)
    return total


def tied(*values):
    return lax.optimization_barrier(values)


def adamw_kernel(place, grads, weights, moments, *refs):
    grads_other, weights_other, moments_other, new_param, new_first, new_second = refs

    def update(core):
        for r in range(2):
            rows = pl.ds(r * HALF, HALF)
            turned = (grads if r == core else grads_other)[...].T
            for c in range(2):
                cols = pl.ds(c * HALF, HALF)
                m = moments if c == core else moments_other
                weight = (weights if c == core else weights_other)[rows, :].astype(f32)
                gradient = turned[:, c * HALF : (c + 1) * HALF]
                first = beta_first * m[rows, :HALF].astype(f32) + (1.0 - beta_first) * gradient
                second = (
                    beta_second * m[rows, HALF:].astype(f32)
                    + (1.0 - beta_second) * gradient * gradient
                )
                step = (
                    first / bias_first / (jnp.sqrt(second / bias_second) + eps_adam)
                    + decay_rate * weight
                )
                new_first[rows, cols] = first
                new_second[rows, cols] = second
                new_param[rows, cols] = (weight - learn_rate * step).astype(bf16)

    for core in range(2):
        pl.when(place[3] == core)(functools.partial(update, core))


def adamw(place, own, other):
    wide = jax.ShapeDtypeStruct((C, C), f32)
    return pl.pallas_call(
        adamw_kernel,
        out_shape=(jax.ShapeDtypeStruct((C, C), bf16), wide, wide),
        in_specs=[SMEM] + [VMEM] * 6,
        out_specs=(VMEM,) * 3,
        compiler_params=pltpu.CompilerParams(vmem_limit_bytes=2**24),
        cost_estimate=LIGHT,
    )(place, *own, *other)


def ordered(index, own, other, axis):
    low = jnp.where(index == 0, own, other)
    high = jnp.where(index == 0, other, own)
    return jnp.concatenate([low, high], axis=axis)


def on_device(tokens, key_grads, old_param, old_first, old_second, old_home):
    f = lax.axis_index("fsdp").astype(jnp.int32)
    d = lax.axis_index("dp").astype(jnp.int32)
    core, zh = d % 2, d // 2
    place = jnp.stack([f % 4, (f // 4) % 4, f // 16, core, zh])

    mine, for_other = split_tokens(place, tokens, key_grads)
    terms = gradient_terms(place, mine, send(for_other, CORE), key_grads)
    far_plus, far_minus, plus_b, minus_a, plus_a, minus_b, stay_a, stay_b = terms

    table, rows_taken = routes(old_home, f, old_param.shape[0] // BR)
    packed = pack(place, table, old_param, old_first, old_second)

    far_plus, far_minus = send(far_plus, OUTER, 1), send(far_minus, OUTER, 3)
    plus_a = add(plus_a, far_plus).astype(bf16)
    minus_b = add(minus_b, far_minus).astype(bf16)
    packed, plus_a, minus_b, plus_b, minus_a = tied(packed, plus_a, minus_b, plus_b, minus_a)
    plus_b, minus_a = send(plus_b, OUTER, 1), send(minus_a, OUTER, 3)
    plus_a, minus_b = send(plus_a, OUTER, 1), send(minus_b, OUTER, 3)
    got = lax.all_to_all(packed, "fsdp", split_axis=0, concat_axis=0, tiled=True)
    seed, moments = unpack(rows_taken, got)
    u = [add(stay_a[s], plus_a[s], minus_a[s]).astype(bf16) for s in range(2)]
    u += [add(stay_b[s], plus_b[s], minus_b[s]).astype(bf16) for s in range(2)]

    two = jnp.stack([seed, send(seed, PAIR)])
    own = jnp.stack([two] + [send(two, INNER, s) for s in (1, 2, 3)])

    own, *u = tied(own, *u)
    got = [send(u[s], INNER, s) for s in (2, 1, 3)]
    plus, minus = send(own, OUTER, 1), send(own, OUTER, 3)
    away = add(u[0][1], *[g[1] for g in got]).astype(bf16)
    away, plus, minus = tied(away, plus, minus)
    got_away = send(away, PAIR)
    far = (send(plus[:2], OUTER, 1), send(minus[2:], OUTER, 3))
    near = (own, plus, minus)
    near_other = tuple(send(p, CORE) for p in near)
    partial = add(u[0][0], *[g[0] for g in got], got_away).astype(bf16)

    partial, *near_other = tied(partial, *near_other)
    near_other = tuple(near_other)
    replica = send(partial, REPLICA)
    start, near_grads = near_products(place, tokens, key_grads, near + near_other)
    gradient = partial.astype(f32) + replica.astype(f32)
    *far, gradient, start = tied(*far, gradient, start)
    far = tuple(far)
    far_other = tuple(send(p, CORE) for p in far)
    gradient_other = send(gradient, CORE)
    keys, input_grads = far_products(
        place, tokens, key_grads, start, near_grads, near + far + near_other + far_other
    )

    moments_zh = send(moments, REPLICA)
    halves = jnp.concatenate(
        [
            ordered(zh, moments[:, :QUARTER], moments_zh[:, :QUARTER], 1),
            ordered(zh, moments[:, QUARTER:], moments_zh[:, QUARTER:], 1),
        ],
        axis=1,
    )
    halves_other = send(halves, CORE)
    seed_other = near_other[0][0, 0]

    new_param, new_first, new_second = adamw(
        place, (gradient, seed, halves), (gradient_other, seed_other, halves_other)
    )
    return (keys, input_grads, new_param, new_first, new_second)


def solution(mesh):
    over_all = P(("fsdp", "dp"), None)
    over_fsdp = P("fsdp", None)
    return jax.shard_map(
        on_device,
        mesh=mesh,
        in_specs=(over_all, over_all, over_fsdp, over_fsdp, over_fsdp, P()),
        out_specs=(over_all, over_all, over_fsdp, over_fsdp, over_fsdp),
        check_vma=False,
    )
```

```python
import functools
import itertools

import jax
import jax.numpy as jnp
from jax import lax
from jax.experimental import pallas as pl
from jax.experimental.pallas import tpu as pltpu
from jax.sharding import PartitionSpec as P

BR = 16
C = 512
HALF = 256
QUARTER = 128
TOK = 256
D = 16384
NF = 32

beta_first = 0.9
beta_second = 0.95
eps_adam = 1e-08
learn_rate = 0.001
decay_rate = 0.1
bias_first = 1.0 - 0.9**10
bias_second = 1.0 - 0.95**10

AXES = ("fsdp", "dp")
bf16 = jnp.bfloat16
f32 = jnp.float32
ANY = pl.BlockSpec(memory_space=pl.ANY)
SMEM = pl.BlockSpec(memory_space=pltpu.SMEM)
VMEM = pl.BlockSpec(memory_space=pltpu.VMEM)
LIGHT = pl.CostEstimate(flops=0, bytes_accessed=1024, transcendentals=0)


def device_number(x, y, zl, zh, core):
    return (((zl * 4 + y) * 4 + x) * 2 + zh) * 2 + core


def shift_pairs(axis_of_core, shift):
    pairs = []
    for x, y, zl, zh, core in itertools.product(range(4), range(4), range(2), range(2), range(2)):
        to = {"x": x, "y": y, "l": zl, "h": zh, "c": core}
        axis = axis_of_core[core]
        to[axis] = (to[axis] + shift) % (4 if axis in "xy" else 2)
        pairs.append(
            (
                device_number(x, y, zl, zh, core),
                device_number(to["x"], to["y"], to["l"], to["h"], to["c"]),
            )
        )
    return pairs


def send(array, axis_of_core, shift=1):
    return lax.ppermute(array, AXES, shift_pairs(axis_of_core, shift))


OUTER = "xy"
INNER = "yx"
PAIR = "ll"
REPLICA = "hh"
CORE = "cc"


def split_kernel(place, tokens, key_grads, out):
    core = place[3]
    for i in range(NF):
        at = pl.multiple_of(i * C + (1 - core) * HALF, HALF)
        out[:, i * HALF : (i + 1) * HALF] = tokens[:, pl.ds(at, HALF)]
    out[:, D // 2 :] = key_grads[...]


def split_tokens(place, tokens, key_grads):
    return pl.pallas_call(
        split_kernel,
        out_shape=jax.ShapeDtypeStruct((TOK, D // 2 + C), bf16),
        in_specs=[SMEM, VMEM, VMEM],
        out_specs=VMEM,
        compiler_params=pltpu.CompilerParams(vmem_limit_bytes=40 * 2**20),
        cost_estimate=LIGHT,
    )(place, tokens, key_grads)


def pack_kernel(place, table, param, first, second, out):
    def body(k, carry):
        src = pl.multiple_of(table[k] * BR, BR)
        dst = pl.multiple_of(k * BR, BR)
        out[pl.ds(dst, BR), :HALF] = param[pl.ds(src, BR), :]
        out[pl.ds(dst, BR), HALF : HALF + QUARTER] = first[pl.ds(src, BR), :].astype(bf16)
        out[pl.ds(dst, BR), HALF + QUARTER :] = second[pl.ds(src, BR), :].astype(bf16)
        return carry

    lax.fori_loop(0, 2 * NF, body, 0, unroll=4)


def pack(place, table, param, first, second):
    rows = param.shape[0]
    quarter = lambda i, place, table: (0, place[3] * 2 + place[4])
    return pl.pallas_call(
        pack_kernel,
        out_shape=jax.ShapeDtypeStruct((2 * NF * BR, C), bf16),
        grid_spec=pltpu.PrefetchScalarGridSpec(
            num_scalar_prefetch=2,
            grid=(1,),
            in_specs=[
                pl.BlockSpec((rows, HALF), lambda i, place, table: (0, place[3])),
                pl.BlockSpec((rows, QUARTER), quarter),
                pl.BlockSpec((rows, QUARTER), quarter),
            ],
            out_specs=pl.BlockSpec((2 * NF * BR, C), lambda i, place, table: (0, 0)),
        ),
        compiler_params=pltpu.CompilerParams(vmem_limit_bytes=2**24),
        cost_estimate=LIGHT,
    )(place, table, param, first, second)


def unpack_kernel(rows_taken, got, weight, moments):
    def body(k, carry):
        src = pl.multiple_of(rows_taken[k] * BR, BR)
        dst = pl.multiple_of(k * BR, BR)
        weight[pl.ds(dst, BR), :] = got[pl.ds(src, BR), :HALF]
        moments[pl.ds(dst, BR), :] = got[pl.ds(src, BR), HALF:]
        return carry

    lax.fori_loop(0, NF, body, 0, unroll=4)


def unpack(rows_taken, got):
    half = jax.ShapeDtypeStruct((C, HALF), bf16)
    return pl.pallas_call(
        unpack_kernel,
        out_shape=(half, half),
        in_specs=[SMEM, VMEM],
        out_specs=(VMEM, VMEM),
        compiler_params=pltpu.CompilerParams(vmem_limit_bytes=2**23),
        cost_estimate=LIGHT,
    )(rows_taken, got)


def target_index(place, core, outer, pair, inner, sign):
    x, y, zl = place[0], place[1], place[2]
    along_x = jnp.where(core == 0, outer, inner)
    along_y = jnp.where(core == 0, inner, outer)
    to_x = lax.rem(x + sign * along_x + 4, 4)
    to_y = lax.rem(y + sign * along_y + 4, 4)
    to_z = lax.rem(zl + pair, 2)
    return (to_z * 4 + to_y) * 4 + to_x


def gradient_term(place, tokens, theirs, grads_t, outer, inner, pair):
    core = place[3]
    f = target_index(place, core, outer, pair, inner, 1)
    mine = tokens[:, pl.ds(pl.multiple_of(f * C + core * HALF, HALF), HALF)]
    other = theirs[:, pl.ds(pl.multiple_of(f * HALF, HALF), HALF)]
    return jnp.dot(
        grads_t[...], jnp.concatenate([mine, other], axis=0), preferred_element_type=f32
    )


def first_gradient_kernel(place, tokens, theirs, key_grads, *refs):
    outs, grads_t = refs[:6], refs[6]
    grads_t[:, :TOK] = key_grads[...].T
    grads_t[:, TOK:] = theirs[:, D // 2 :].T
    halves = ((2, 0), (2, 2), (1, 2), (3, 0), (0, 0), (0, 2))
    for ref, (outer, first) in zip(outs, halves):

        def body(inner, carry, ref=ref, outer=outer, first=first):
            for pair in range(2):
                ref[inner, pair] = gradient_term(
                    place, tokens, theirs, grads_t, outer, first + inner, pair
                ).astype(bf16)
            return carry

        lax.fori_loop(0, 2, body, 0, unroll=2)


def joined_gradient_kernel(place, tokens, theirs, grads_t, far_plus, far_minus, plus, minus):
    for ref, far, outer, first in ((plus, far_plus, 1, 0), (minus, far_minus, 3, 2)):
        for inner in range(2):
            for pair in range(2):
                term = gradient_term(place, tokens, theirs, grads_t, outer, first + inner, pair)
                ref[inner, pair] = (term + far[inner, pair].astype(f32)).astype(bf16)


def gradient_call(kernel, halves, others, cost, *args):
    half = jax.ShapeDtypeStruct((2, 2, C, HALF), bf16)
    return pl.pallas_call(
        kernel,
        out_shape=(half,) * halves + others,
        in_specs=[SMEM] + [VMEM] * (len(args) - 1),
        out_specs=(VMEM,) * (halves + len(others)),
        compiler_params=pltpu.CompilerParams(vmem_limit_bytes=24 * 2**20),
        cost_estimate=cost,
    )(*args)


def is_near(outer, inner):
    return outer != 2 and inner != 2


def products(place, tokens, key_grads, piece, near, total, scratch, input_grads, start):
    held, weights, made, sem_in, sem_w, sem = scratch
    core = place[3]
    turn = lambda k: pl.ds(pl.multiple_of(k * HALF, HALF), HALF)
    steps = [
        (outer, inner, pair)
        for outer in range(4)
        for inner in range(4)
        for pair in range(2)
        if is_near(outer, inner) == near
    ]
    spots, loads = [], []
    for k, (outer, inner, pair) in enumerate(steps):
        f = target_index(place, core, outer, pair, inner, -1)
        spots.append(pl.ds(pl.multiple_of(f * C, C), C))
        sources = (piece(0, outer, inner, pair), piece(1, inner, outer, pair))
        loads.append(
            [
                pltpu.make_async_copy(sources[of], weights.at[k, of], sem_w.at[of, k])
                for of in range(2)
            ]
            + [pltpu.make_async_copy(tokens.at[:, spots[k]], held.at[k], sem_in.at[k])]
        )
        for copy in loads[k]:
            copy.start()
    grads = jnp.concatenate([key_grads[:, turn(core)], key_grads[:, turn(1 - core)]], axis=1)
    for k in range(len(steps)):
        for copy in loads[k]:
            copy.wait()
        weight = jnp.concatenate([weights[k, 0], weights[k, 1]], axis=1)
        made[k] = lax.dot_general(
            grads, weight, (((1,), (1,)), ((), ())), preferred_element_type=f32
        ).astype(bf16)
        pltpu.make_async_copy(made.at[k], input_grads.at[:, spots[k]], sem).start()
        term = jnp.dot(held[k], weight, preferred_element_type=f32)
        if k == 0:
            total[...] = term if start is None else start[...] + term
        else:
            total[...] += term
    pltpu.make_async_copy(made, made, sem).wait()


def piece_of(arrays, per_core):
    which = {0: 0, 1: 1, 3: 2}

    def piece(of, outer, inner, pair):
        if outer == 2:
            return arrays[per_core * of + 3 + inner // 2].at[inner % 2, pair]
        return arrays[per_core * of + which[outer]].at[inner, pair]

    return piece


def near_kernel(place, tokens, key_grads, *refs):
    arrays, (total, input_grads, *scratch) = refs[:6], refs[6:]
    piece = piece_of(arrays, 3)
    products(place, tokens, key_grads, piece, True, total, scratch, input_grads, None)


def far_kernel(place, tokens, key_grads, start, near_grads, *refs):
    arrays, (keys, input_grads, total, *scratch) = refs[:10], refs[10:]
    piece = piece_of(arrays, 5)
    products(place, tokens, key_grads, piece, False, total, scratch, input_grads, start)
    core = place[3]
    for of in range(2):
        owner = core if of == 0 else 1 - core
        keys[:, pl.ds(pl.multiple_of(owner * HALF, HALF), HALF)] = total[
            :, of * HALF : (of + 1) * HALF
        ].astype(bf16)


def product_scratch(steps):
    return [
        pltpu.VMEM((steps, TOK, C), bf16),
        pltpu.VMEM((steps, 2, C, HALF), bf16),
        pltpu.VMEM((steps, TOK, C), bf16),
        pltpu.SemaphoreType.DMA((steps,)),
        pltpu.SemaphoreType.DMA((2, steps)),
        pltpu.SemaphoreType.DMA,
    ]


def near_products(place, tokens, key_grads, pieces):
    return pl.pallas_call(
        near_kernel,
        out_shape=(
            jax.ShapeDtypeStruct((TOK, C), f32),
            jax.ShapeDtypeStruct((TOK, D), bf16),
        ),
        in_specs=[SMEM, ANY, VMEM] + [ANY] * 6,
        out_specs=(VMEM, ANY),
        scratch_shapes=product_scratch(18),
        compiler_params=pltpu.CompilerParams(vmem_limit_bytes=56 * 2**20),
        cost_estimate=LIGHT,
    )(place, tokens, key_grads, *pieces)


def far_products(place, tokens, key_grads, start, near_grads, pieces):
    return pl.pallas_call(
        far_kernel,
        out_shape=(
            jax.ShapeDtypeStruct((TOK, C), bf16),
            jax.ShapeDtypeStruct((TOK, D), bf16),
        ),
        in_specs=[SMEM, ANY, VMEM, VMEM] + [ANY] * 11,
        out_specs=(VMEM, ANY),
        scratch_shapes=[pltpu.VMEM((TOK, C), f32)] + product_scratch(14),
        input_output_aliases={4: 1},
        compiler_params=pltpu.CompilerParams(vmem_limit_bytes=56 * 2**20),
        cost_estimate=LIGHT,
    )(place, tokens, key_grads, start, near_grads, *pieces)


def routes(old_home, f, slots):
    home = old_home.reshape(NF, NF)
    source = home // slots
    idx = jnp.arange(NF)
    earlier = idx[None, :, None] > idx[None, None, :]
    same = source[:, :, None] == source[:, None, :]
    rank = jnp.sum((same & earlier).astype(jnp.int32), axis=2)
    mine = source == f
    slot = jnp.where(mine, home % slots, 0)
    table = jnp.stack([jnp.sum(jnp.where(rank == r, slot, 0), axis=1) for r in range(2)], axis=1)
    arrives = source * 2 + rank
    rows_taken = jnp.sum(jnp.where(idx[:, None] == f, arrives, 0), axis=0)
    return table.reshape(2 * NF), rows_taken


def add(*terms):
    total = terms[0].astype(f32)
    for term in terms[1:]:
        total = total + term.astype(f32)
    return total


def tied(*values):
    return lax.optimization_barrier(values)


def adamw_kernel(place, grads, weights, moments, *refs):
    grads_other, weights_other, moments_other, new_param, new_first, new_second = refs

    def update(core):
        for r in range(2):
            rows = pl.ds(r * HALF, HALF)
            turned = (grads if r == core else grads_other)[...].T
            for c in range(2):
                cols = pl.ds(c * HALF, HALF)
                m = moments if c == core else moments_other
                weight = (weights if c == core else weights_other)[rows, :].astype(f32)
                gradient = turned[:, c * HALF : (c + 1) * HALF]
                first = beta_first * m[rows, :HALF].astype(f32) + (1.0 - beta_first) * gradient
                second = (
                    beta_second * m[rows, HALF:].astype(f32)
                    + (1.0 - beta_second) * gradient * gradient
                )
                step = (
                    first / bias_first / (jnp.sqrt(second / bias_second) + eps_adam)
                    + decay_rate * weight
                )
                new_first[rows, cols] = first
                new_second[rows, cols] = second
                new_param[rows, cols] = (weight - learn_rate * step).astype(bf16)

    for core in range(2):
        pl.when(place[3] == core)(functools.partial(update, core))


def adamw(place, own, other):
    wide = jax.ShapeDtypeStruct((C, C), f32)
    return pl.pallas_call(
        adamw_kernel,
        out_shape=(jax.ShapeDtypeStruct((C, C), bf16), wide, wide),
        in_specs=[SMEM] + [VMEM] * 6,
        out_specs=(VMEM,) * 3,
        compiler_params=pltpu.CompilerParams(vmem_limit_bytes=2**24),
        cost_estimate=LIGHT,
    )(place, *own, *other)


def ordered(index, own, other, axis):
    low = jnp.where(index == 0, own, other)
    high = jnp.where(index == 0, other, own)
    return jnp.concatenate([low, high], axis=axis)


def on_device(tokens, key_grads, old_param, old_first, old_second, old_home):
    f = lax.axis_index("fsdp").astype(jnp.int32)
    d = lax.axis_index("dp").astype(jnp.int32)
    core, zh = d % 2, d // 2
    place = jnp.stack([f % 4, (f // 4) % 4, f // 16, core, zh])

    theirs = send(split_tokens(place, tokens, key_grads), CORE)
    table, rows_taken = routes(old_home, f, old_param.shape[0] // BR)
    packed = pack(place, table, old_param, old_first, old_second)
    theirs, packed = tied(theirs, packed)

    turned = (jax.ShapeDtypeStruct((C, 2 * TOK), bf16),)
    far_plus, far_minus, plus_b, minus_a, stay_a, stay_b, grads_t = gradient_call(
        first_gradient_kernel, 6, turned, LIGHT, place, tokens, theirs, key_grads
    )
    packed, far_plus, far_minus, plus_b, minus_a = tied(
        packed, far_plus, far_minus, plus_b, minus_a
    )
    far_plus, far_minus = send(far_plus, OUTER, 1), send(far_minus, OUTER, 3)
    plus_b, minus_a = send(plus_b, OUTER, 1), send(minus_a, OUTER, 3)
    got = lax.all_to_all(packed, "fsdp", split_axis=0, concat_axis=0, tiled=True)
    seed, moments = unpack(rows_taken, got)
    seed, plus_b, minus_a, far_plus, far_minus = tied(seed, plus_b, minus_a, far_plus, far_minus)
    plus_a, minus_b = gradient_call(
        joined_gradient_kernel, 2, (), LIGHT, place, tokens, theirs, grads_t, far_plus, far_minus
    )
    two = jnp.stack([seed, send(seed, PAIR)])
    two, plus_a, minus_b = tied(two, plus_a, minus_b)
    plus_a, minus_b = send(plus_a, OUTER, 1), send(minus_b, OUTER, 3)
    u = [add(stay_a[s], plus_a[s], minus_a[s]).astype(bf16) for s in range(2)]
    u += [add(stay_b[s], plus_b[s], minus_b[s]).astype(bf16) for s in range(2)]

    own = jnp.stack([two] + [send(two, INNER, s) for s in (1, 2, 3)])

    own, *u = tied(own, *u)
    got = [send(u[s], INNER, s) for s in (2, 1, 3)]
    plus, minus = send(own, OUTER, 1), send(own, OUTER, 3)
    away = add(u[0][1], *[g[1] for g in got]).astype(bf16)
    away, plus, minus = tied(away, plus, minus)
    got_away = send(away, PAIR)
    far = (send(plus[:2], OUTER, 1), send(minus[2:], OUTER, 3))
    near = (own, plus, minus)
    near_other = tuple(send(p, CORE) for p in near)
    partial = add(u[0][0], *[g[0] for g in got], got_away).astype(bf16)

    partial, *near_other = tied(partial, *near_other)
    near_other = tuple(near_other)
    replica = send(partial, REPLICA)
    start, near_grads = near_products(place, tokens, key_grads, near + near_other)
    gradient = partial.astype(f32) + replica.astype(f32)
    *far, gradient, start = tied(*far, gradient, start)
    far = tuple(far)
    far_other = tuple(send(p, CORE) for p in far)
    gradient_other = send(gradient, CORE)
    keys, input_grads = far_products(
        place, tokens, key_grads, start, near_grads, near + far + near_other + far_other
    )

    moments_zh = send(moments, REPLICA)
    halves = jnp.concatenate(
        [
            ordered(zh, moments[:, :QUARTER], moments_zh[:, :QUARTER], 1),
            ordered(zh, moments[:, QUARTER:], moments_zh[:, QUARTER:], 1),
        ],
        axis=1,
    )
    halves_other = send(halves, CORE)
    seed_other = near_other[0][0, 0]

    new_param, new_first, new_second = adamw(
        place, (gradient, seed, halves), (gradient_other, seed_other, halves_other)
    )
    return (keys, input_grads, new_param, new_first, new_second)


def solution(mesh):
    over_all = P(("fsdp", "dp"), None)
    over_fsdp = P("fsdp", None)
    return jax.shard_map(
        on_device,
        mesh=mesh,
        in_specs=(over_all, over_all, over_fsdp, over_fsdp, over_fsdp, P()),
        out_specs=(over_all, over_all, over_fsdp, over_fsdp, over_fsdp),
        check_vma=False,
    )
```
